512 devices in a mesh: dp: 32 (over z_hi, x, core), tensor: 16 (over y, z_lo).
Axes of the slice: x: 4, y: 8, z: 8 (z_hi: 4, z_lo: 2; z = z_hi * 2 + z_lo), core: 2. Of those that a mesh axis runs over, the one named last changes fastest.
Arguments:
- tokens: bfloat16 [512, 8192], P('tensor', 'dp'), may hold values from -6 to 6
- weight_in: bfloat16 [8192, 16384], P('dp', 'tensor'), may hold values from -0.0625 to 0.0625
- tangent_in: bfloat16 [8192, 16384], P('dp', 'tensor'), may hold values from -0.0625 to 0.0625
- weight_out: bfloat16 [16384, 8192], P('tensor', 'dp'), may hold values from -0.046875 to 0.046875
- tangent_out: bfloat16 [16384, 8192], P('tensor', 'dp'), may hold values from -0.046875 to 0.046875
- curvature: float32 [512, 8192], P('tensor', 'dp'), may hold values from 0.02 to 0.2
Outputs:
- product_in: bfloat16 [8192, 16384], P('dp', 'tensor')
- product_out: bfloat16 [16384, 8192], P('tensor', 'dp')
The draws below stay inside these ranges and needn't reach their ends.
All inputs are finite; a program needn't handle non-finite values.
Results may differ from the reference program's by a relative error of at most 0.035.
Values may be sent and summed in bfloat16 or wider, within the bound.
No kernel may reach another device: no remote copies, remote signals or barrier semaphores. Data moves between devices by JAX's collectives and lax.ppermute only.
A program may use at most 64 MiB of HBM per device.

```python
import math
import jax
import jax.numpy as jnp
from jax import lax

D = 8192
F = 16384
TOKENS = 512
N_DP = 32


def block_scale(own_key, dims, shards, least, largest):
    def one(axis_at, shards_of):
        draws = jax.random.uniform(jax.random.fold_in(jax.random.fold_in(own_key, 6), axis_at), (shards_of,), jnp.float32, least / len(shards), largest / len(shards))
        return jnp.repeat(jnp.exp(draws), dims[axis_at] // shards_of).reshape((-1,) + (1,) * (len(dims) - axis_at - 1))

    factor_of = one(*shards[0])
    for cut in shards[1:]:
        factor_of = factor_of * one(*cut)
    return factor_of


def centred(key, extent, deviation, most, pieces=(), kind=jnp.bfloat16):
    drawn = deviation * jax.random.normal(key, extent, jnp.float32)
    if pieces:
        drawn = drawn * block_scale(key, extent, pieces, -0.22, 0.18)
    return jnp.clip(drawn, -most, most).astype(kind)


def setup_inputs(seed: int = 0) -> dict:
    key_of = jax.random.split(jax.random.key(seed), 7)
    tokens = centred(key_of[0], (TOKENS, D), 1.0, 6.0, ((0, 16), (1, 32)))
    weight_in = centred(key_of[1], (D, F), D ** -0.5, 0.0625, ((0, 32), (1, 16)))
    tangent_in = centred(key_of[2], (D, F), D ** -0.5, 0.0625, ((0, 32), (1, 16)))
    weight_out = centred(key_of[3], (F, D), F ** -0.5, 0.046875, ((0, 16), (1, 32)))
    tangent_out = centred(key_of[4], (F, D), F ** -0.5, 0.046875, ((0, 16), (1, 32)))
    curvature = jnp.clip(jnp.exp(math.log(0.2) - 2.3025851 * jax.random.uniform(key_of[5], (TOKENS, D), jnp.float32) ** block_scale(key_of[5], (TOKENS, D), ((0, 16), (1, 32)), -0.2, 0.2)), 0.02, 0.2)
    return {"tokens": tokens, "weight_in": weight_in, "tangent_in": tangent_in, "weight_out": weight_out, "tangent_out": tangent_out, "curvature": curvature}


gelu_scale = math.sqrt(2.0 / math.pi)

def gelu_pair(hidden):
    argument = gelu_scale * (hidden + 0.044715 * hidden * hidden * hidden)
    hyper = jnp.tanh(argument)
    values = 0.5 * hidden * (1.0 + hyper)
    derivative = 0.5 * (1.0 + hyper) + 0.5 * hidden * (1.0 - hyper * hyper) * gelu_scale * (1.0 + 3.0 * 0.044715 * hidden * hidden)
    return (values, derivative)

def block_sum(left_side, right_side):
    blocks = left_side.shape[1] // N_DP
    left_blocks = left_side.reshape(left_side.shape[0], N_DP, blocks).transpose(1, 0, 2)
    right_blocks = right_side.reshape(N_DP, blocks, right_side.shape[1])

    def accumulate(summed, operands):
        partial_value = jnp.dot(operands[0], operands[1], preferred_element_type=jnp.float32).astype(jnp.bfloat16)
        partial_value = lax.optimization_barrier(partial_value)
        return (summed + partial_value.astype(jnp.float32), None)
    start_sum = jnp.zeros((left_side.shape[0], right_side.shape[1]), jnp.float32)
    summed, unused = lax.scan(accumulate, start_sum, (left_blocks, right_blocks))
    return summed

def reference(tokens, weight_in, tangent_in, weight_out, tangent_out, curvature):
    preact = block_sum(tokens, weight_in)
    tangent_h = block_sum(tokens, tangent_in)
    values, derivative = gelu_pair(preact)
    active = values.astype(jnp.bfloat16)
    moved = (derivative * tangent_h).astype(jnp.bfloat16)
    output_tangent = jnp.dot(moved, weight_out, preferred_element_type=jnp.float32) + jnp.dot(active, tangent_out, preferred_element_type=jnp.float32)
    cotangent = (curvature * output_tangent).astype(jnp.bfloat16)
    product_out = jnp.dot(active.T, cotangent, preferred_element_type=jnp.float32).astype(jnp.bfloat16)
    backward = block_sum(cotangent, weight_out.T)
    hidden_grad = (backward * derivative).astype(jnp.bfloat16)
    product_in = jnp.dot(tokens.T, hidden_grad, preferred_element_type=jnp.float32).astype(jnp.bfloat16)
    return (product_in, product_out)
```

```python
import math

import jax
import jax.numpy as jnp
from jax import lax
from jax.sharding import Mesh
from jax.sharding import PartitionSpec as P

gelu_scale = math.sqrt(2.0 / math.pi)
ROWS = ("zh", "x")
TENSOR = ("y", "zl")
SWAP = [(0, 1), (1, 0)]


def gelu_pair(hidden):
    argument = gelu_scale * (hidden + 0.044715 * hidden * hidden * hidden)
    hyper = jnp.tanh(argument)
    values = 0.5 * hidden * (1.0 + hyper)
    derivative = 0.5 * (1.0 + hyper) + 0.5 * hidden * (1.0 - hyper * hyper) * gelu_scale * (
        1.0 + 3.0 * 0.044715 * hidden * hidden
    )
    return (values, derivative)


def dot(left_side, right_side, left_dim=1, right_dim=0):
    return lax.dot_general(
        left_side,
        right_side,
        (((left_dim,), (right_dim,)), ((), ())),
        preferred_element_type=jnp.float32,
    )


def gather_rows(block, axes):
    count = lax.axis_size(axes)
    copies = jnp.broadcast_to(block[None], (count,) + block.shape)
    copies = copies.reshape(count * block.shape[0], block.shape[1])
    return lax.all_to_all(copies, axes, split_axis=0, concat_axis=0, tiled=True)


def sum_rows(partial, axes):
    count = lax.axis_size(axes)
    pieces = lax.all_to_all(partial, axes, split_axis=0, concat_axis=0, tiled=True)
    pieces = pieces.reshape(count, partial.shape[0] // count, partial.shape[1])
    return jnp.sum(pieces.astype(jnp.float32), axis=0)


def swap_cores(block):
    return lax.ppermute(block, "c", SWAP)


def other_core(block, other):
    both = lax.all_gather(block, "c", axis=0, tiled=False)
    return lax.dynamic_index_in_dim(both, other, 0, keepdims=False)


def on_device(tokens, weight_in, tangent_in, weight_out, tangent_out, curvature):
    core = lax.axis_index("c")
    other = 1 - core
    half = weight_in.shape[1] // 2

    def columns(array, which):
        return lax.dynamic_slice_in_dim(array, which * half, half, 1)

    def rows(array, which):
        return lax.dynamic_slice_in_dim(array, which * half, half, 0)

    pair_own = jnp.concatenate([columns(weight_in, core), columns(tangent_in, core)], axis=1)
    pair_far = swap_cores(
        jnp.concatenate([columns(weight_in, other), columns(tangent_in, other)], axis=1)
    )
    out_own = rows(weight_out, core)
    out_far = swap_cores(rows(weight_out, other))

    tokens_own = gather_rows(tokens, TENSOR)
    tokens_far = other_core(tokens_own, other)
    joined = (dot(tokens_own, pair_own) + dot(tokens_far, pair_far)).astype(jnp.bfloat16)
    joined = sum_rows(joined, ROWS)
    values, derivative = gelu_pair(joined[:, :half])
    moved = derivative * joined[:, half:]
    both = jnp.concatenate([values, moved], axis=1).astype(jnp.bfloat16)
    both_own = gather_rows(both, ROWS)
    both_far = swap_cores(both_own)

    output_tangent = (
        dot(both_own[:, half:], out_own)
        + dot(both_own[:, :half], rows(tangent_out, core))
        + dot(both_far[:, half:], rows(weight_out, other))
        + dot(both_far[:, :half], rows(tangent_out, other))
    ).astype(jnp.bfloat16)
    output_tangent = sum_rows(output_tangent, TENSOR)
    cotangent = (curvature * output_tangent).astype(jnp.bfloat16)
    cotangent_own = gather_rows(cotangent, TENSOR)
    cotangent_far = other_core(cotangent_own, other)

    backward = (
        dot(cotangent_own, out_own, 1, 1) + dot(cotangent_far, out_far, 1, 1)
    ).astype(jnp.bfloat16)
    backward = sum_rows(backward, ROWS)
    first = jnp.where(core == 0, both_own[:, :half], both_far[:, :half])
    second = jnp.where(core == 0, both_far[:, :half], both_own[:, :half])
    product_out = jnp.concatenate(
        [dot(first, cotangent_own, 0, 0), dot(second, cotangent_own, 0, 0)], axis=0
    ).astype(jnp.bfloat16)

    hidden_grad = (backward * derivative).astype(jnp.bfloat16)
    grad_own = gather_rows(hidden_grad, ROWS)
    grad_far = swap_cores(grad_own)
    first = jnp.where(core == 0, grad_own, grad_far)
    second = jnp.where(core == 0, grad_far, grad_own)
    product_in = jnp.concatenate(
        [dot(tokens_own, first, 0, 0), dot(tokens_own, second, 0, 0)], axis=1
    ).astype(jnp.bfloat16)
    return (product_in, product_out)


def solution(mesh):
    fine = Mesh(mesh.devices.reshape(4, 4, 2, 8, 2), ("zh", "x", "c", "y", "zl"))
    by_dp = ("zh", "x", "c")
    return jax.shard_map(
        on_device,
        mesh=fine,
        in_specs=(
            P(TENSOR, by_dp),
            P(by_dp, TENSOR),
            P(by_dp, TENSOR),
            P(TENSOR, by_dp),
            P(TENSOR, by_dp),
            P(TENSOR, by_dp),
        ),
        out_specs=(P(by_dp, TENSOR), P(TENSOR, by_dp)),
        check_vma=False,
    )
```

```python
import math

import jax
import jax.numpy as jnp
from jax import lax
from jax.sharding import Mesh
from jax.sharding import PartitionSpec as P

gelu_scale = math.sqrt(2.0 / math.pi)
ROWS = ("zh", "x")
TENSOR = ("y", "zl")
SWAP = [(0, 1), (1, 0)]


def gelu_pair(hidden):
    argument = gelu_scale * (hidden + 0.044715 * hidden * hidden * hidden)
    hyper = jnp.tanh(argument)
    values = 0.5 * hidden * (1.0 + hyper)
    derivative = 0.5 * (1.0 + hyper) + 0.5 * hidden * (1.0 - hyper * hyper) * gelu_scale * (
        1.0 + 3.0 * 0.044715 * hidden * hidden
    )
    return (values, derivative)


def dot(left_side, right_side, left_dim=1, right_dim=0):
    return lax.dot_general(
        left_side,
        right_side,
        (((left_dim,), (right_dim,)), ((), ())),
        preferred_element_type=jnp.float32,
    )


def gather_rows(block, axes):
    count = lax.axis_size(axes)
    copies = jnp.broadcast_to(block[None], (count,) + block.shape)
    copies = copies.reshape(count * block.shape[0], block.shape[1])
    return lax.all_to_all(copies, axes, split_axis=0, concat_axis=0, tiled=True)


def sum_rows(partial, axes):
    count = lax.axis_size(axes)
    pieces = lax.all_to_all(partial, axes, split_axis=0, concat_axis=0, tiled=True)
    pieces = pieces.reshape(count, partial.shape[0] // count, partial.shape[1])
    return jnp.sum(pieces.astype(jnp.float32), axis=0)


def swap_cores(block):
    return lax.ppermute(block, "c", SWAP)


def on_device(tokens, weight_in, tangent_in, weight_out, tangent_out, curvature):
    core = lax.axis_index("c")
    hidden = weight_in.shape[1]
    features = tokens.shape[1]
    share = tokens.shape[0] // 2

    def rows(array, which):
        return lax.dynamic_slice_in_dim(array, which * share, share, 0)

    def both_cores(array, axis):
        return jnp.concatenate([array, swap_cores(array)], axis=axis)

    def my_rows(array):
        mine = rows(array, core)
        return jnp.concatenate([mine, swap_cores(rows(array, 1 - core))], axis=1)

    tokens_all = gather_rows(my_rows(tokens), TENSOR)
    scale = my_rows(curvature)
    pair = both_cores(jnp.concatenate([weight_in, tangent_in], axis=1), 0)
    out_both = both_cores(weight_out, 1)
    tangent_both = both_cores(tangent_out, 1)

    joined = sum_rows(dot(tokens_all, pair).astype(jnp.bfloat16), ROWS)
    values, derivative = gelu_pair(joined[:, :hidden])
    moved = derivative * joined[:, hidden:]
    both = gather_rows(jnp.concatenate([values, moved], axis=1).astype(jnp.bfloat16), ROWS)
    active = both[:, :hidden]

    output_tangent = dot(both[:, hidden:], out_both) + dot(active, tangent_both)
    output_tangent = sum_rows(output_tangent.astype(jnp.bfloat16), TENSOR)
    cotangent = gather_rows((scale * output_tangent).astype(jnp.bfloat16), TENSOR)

    backward = sum_rows(dot(cotangent, out_both, 1, 1).astype(jnp.bfloat16), ROWS)
    far_out = swap_cores(dot(active, cotangent[:, features:], 0, 0).astype(jnp.bfloat16))
    product_out = dot(active, cotangent[:, :features], 0, 0) + far_out.astype(jnp.float32)

    hidden_grad = gather_rows((backward * derivative).astype(jnp.bfloat16), ROWS)
    far_in = swap_cores(dot(tokens_all[:, features:], hidden_grad, 0, 0).astype(jnp.bfloat16))
    product_in = dot(tokens_all[:, :features], hidden_grad, 0, 0) + far_in.astype(jnp.float32)
    return (product_in.astype(jnp.bfloat16), product_out.astype(jnp.bfloat16))


def solution(mesh):
    fine = Mesh(mesh.devices.reshape(4, 4, 2, 8, 2), ("zh", "x", "c", "y", "zl"))
    by_dp = ("zh", "x", "c")
    return jax.shard_map(
        on_device,
        mesh=fine,
        in_specs=(
            P(TENSOR, by_dp),
            P(by_dp, TENSOR),
            P(by_dp, TENSOR),
            P(TENSOR, by_dp),
            P(TENSOR, by_dp),
            P(TENSOR, by_dp),
        ),
        out_specs=(P(by_dp, TENSOR), P(TENSOR, by_dp)),
        check_vma=False,
    )
```

```python
import math

import jax
import jax.numpy as jnp
from jax import lax
from jax.sharding import Mesh
from jax.sharding import PartitionSpec as P

gelu_scale = math.sqrt(2.0 / math.pi)
ROWS = ("x", "zh")
TENSOR = ("y", "zl")
SWAP = [(0, 1), (1, 0)]


def gelu_pair(hidden):
    argument = gelu_scale * (hidden + 0.044715 * hidden * hidden * hidden)
    hyper = jnp.tanh(argument)
    values = 0.5 * hidden * (1.0 + hyper)
    derivative = 0.5 * (1.0 + hyper) + 0.5 * hidden * (1.0 - hyper * hyper) * gelu_scale * (
        1.0 + 3.0 * 0.044715 * hidden * hidden
    )
    return (values, derivative)


def dot(left_side, right_side, left_dim=1, right_dim=0):
    return lax.dot_general(
        left_side,
        right_side,
        (((left_dim,), (right_dim,)), ((), ())),
        preferred_element_type=jnp.float32,
    )


def exchange(pieces, axes):
    return lax.all_to_all(pieces, axes, split_axis=0, concat_axis=0, tiled=True)


def gather_rows(block, axes):
    count = lax.axis_size(axes)
    copies = jnp.broadcast_to(block[None], (count,) + block.shape)
    return exchange(copies.reshape(count * block.shape[0], block.shape[1]), axes)


def sum_rows(partial, axes):
    count = lax.axis_size(axes)
    pieces = exchange(partial, axes)
    pieces = pieces.reshape(count, partial.shape[0] // count, partial.shape[1])
    return jnp.sum(pieces.astype(jnp.float32), axis=0)


def sum_rows_staged(partial):
    return sum_rows(sum_rows(partial, ("x",)).astype(jnp.bfloat16), ("zh",))


def gather_rows_staged(block):
    return gather_rows(gather_rows(block, ("zh",)), ("x",))


def swap_cores(block):
    return lax.ppermute(block, "c", SWAP)


def on_device(tokens, weight_in, tangent_in, weight_out, tangent_out, curvature):
    core = lax.axis_index("c")
    first_core = core == 0
    hidden = weight_in.shape[1]
    features = tokens.shape[1]
    share = tokens.shape[0] // 2

    halves = tokens.reshape(2, 1, share, features)
    copies = jnp.broadcast_to(halves, (2, lax.axis_size(TENSOR), share, features))
    arrived = exchange(copies.reshape(-1, features), ("c",) + TENSOR).reshape(2, -1, features)
    tokens_own = lax.dynamic_index_in_dim(arrived, core, 0, keepdims=False)
    tokens_far = lax.dynamic_index_in_dim(arrived, 1 - core, 0, keepdims=False)

    in_own = jnp.concatenate([weight_in, tangent_in], axis=1)
    in_far = swap_cores(in_own)
    out_own = jnp.concatenate([weight_out, tangent_out], axis=0)
    out_far = swap_cores(out_own)
    scale_own = lax.dynamic_slice_in_dim(curvature, core * share, share, 0)
    scale_far = swap_cores(lax.dynamic_slice_in_dim(curvature, (1 - core) * share, share, 0))

    joined = (dot(tokens_own, in_own) + dot(tokens_far, in_far)).astype(jnp.bfloat16)
    joined, out_far, scale_far = lax.optimization_barrier((joined, out_far, scale_far))
    joined = lax.cond(first_core, sum_rows_staged, lambda p: sum_rows(p, ROWS), joined)
    values, derivative = gelu_pair(joined[:, :hidden])
    moved = derivative * joined[:, hidden:]
    both = jnp.concatenate([moved, values], axis=1).astype(jnp.bfloat16)
    both = lax.cond(first_core, lambda b: gather_rows(b, ROWS), gather_rows_staged, both)
    active = both[:, hidden:]

    output_tangent = jnp.concatenate([dot(both, out_own), dot(both, out_far)], axis=1)
    output_tangent = sum_rows(output_tangent.astype(jnp.bfloat16), TENSOR)
    scale = jnp.concatenate([scale_own, scale_far], axis=1)
    cotangent = gather_rows((scale * output_tangent).astype(jnp.bfloat16), TENSOR)
    cotangent_own, cotangent_far = cotangent[:, :features], cotangent[:, features:]

    backward = dot(cotangent_own, weight_out, 1, 1) + dot(cotangent_far, out_far[:hidden], 1, 1)
    backward = sum_rows(backward.astype(jnp.bfloat16), ROWS)
    far_out = swap_cores(dot(active, cotangent_far, 0, 0).astype(jnp.bfloat16))
    product_out = dot(active, cotangent_own, 0, 0) + far_out.astype(jnp.float32)

    hidden_grad = gather_rows((backward * derivative).astype(jnp.bfloat16), ROWS)
    far_in = swap_cores(dot(tokens_far, hidden_grad, 0, 0).astype(jnp.bfloat16))
    product_in = dot(tokens_own, hidden_grad, 0, 0) + far_in.astype(jnp.float32)
    return (product_in.astype(jnp.bfloat16), product_out.astype(jnp.bfloat16))


def solution(mesh):
    fine = Mesh(mesh.devices.reshape(4, 4, 2, 8, 2), ("zh", "x", "c", "y", "zl"))
    by_dp = ("zh", "x", "c")
    return jax.shard_map(
        on_device,
        mesh=fine,
        in_specs=(
            P(TENSOR, by_dp),
            P(by_dp, TENSOR),
            P(by_dp, TENSOR),
            P(TENSOR, by_dp),
            P(TENSOR, by_dp),
            P(TENSOR, by_dp),
        ),
        out_specs=(P(by_dp, TENSOR), P(TENSOR, by_dp)),
        check_vma=False,
    )
```

```python
import math

import jax
import jax.numpy as jnp
from jax import lax
from jax.experimental import pallas as pl
from jax.experimental.pallas import tpu as pltpu
from jax.sharding import Mesh
from jax.sharding import PartitionSpec as P

gelu_scale = math.sqrt(2.0 / math.pi)
ROWS = ("x", "zh")
TENSOR = ("y", "zl")
SWAP = [(0, 1), (1, 0)]


def gelu_pair(hidden):
    argument = gelu_scale * (hidden + 0.044715 * hidden * hidden * hidden)
    hyper = jnp.tanh(argument)
    values = 0.5 * hidden * (1.0 + hyper)
    derivative = 0.5 * (1.0 + hyper) + 0.5 * hidden * (1.0 - hyper * hyper) * gelu_scale * (
        1.0 + 3.0 * 0.044715 * hidden * hidden
    )
    return (values, derivative)


def dot(left_side, right_side, left_dim=1, right_dim=0):
    return lax.dot_general(
        left_side,
        right_side,
        (((left_dim,), (right_dim,)), ((), ())),
        preferred_element_type=jnp.float32,
    )


def exchange(pieces, axes):
    return lax.all_to_all(pieces, axes, split_axis=0, concat_axis=0, tiled=True)


IN_VMEM = pl.BlockSpec(memory_space=pltpu.VMEM)


def kernel_call(kernel, results, operands, flops):
    moved_bytes = sum(x.size * x.dtype.itemsize for x in (*results, *operands))
    return pl.pallas_call(
        kernel,
        out_shape=results,
        in_specs=[IN_VMEM] * len(operands),
        out_specs=[IN_VMEM] * len(results),
        compiler_params=pltpu.CompilerParams(vmem_limit_bytes=16 * 2**20),
        cost_estimate=pl.CostEstimate(flops=flops, bytes_accessed=moved_bytes, transcendentals=0),
    )(*operands)


def far_products_kernel(far_ref, in_far_ref, slope_far_ref, preact_ref, tangent_ref, result_ref):
    hidden = in_far_ref.shape[1]
    far = far_ref[...]
    preact = preact_ref[...] + dot(far, in_far_ref[...])
    result_ref[:, :hidden] = preact.astype(result_ref.dtype)
    tangent = tangent_ref[...] + dot(far, slope_far_ref[...])
    result_ref[:, hidden:] = tangent.astype(result_ref.dtype)


def both_products_kernel(both_ref, out_ref, turn_ref, out_far_ref, turn_far_ref, result_ref):
    hidden, width = out_ref.shape
    moved, active = both_ref[:, :hidden], both_ref[:, hidden:]
    own = dot(moved, out_ref[...]) + dot(active, turn_ref[...])
    result_ref[:, :width] = own.astype(result_ref.dtype)
    far = dot(moved, out_far_ref[...]) + dot(active, turn_far_ref[...])
    result_ref[:, width:] = far.astype(result_ref.dtype)


def sum_pieces(pieces_ref):
    return jnp.sum(pieces_ref[...].astype(jnp.float32), axis=0)


def partial_sum_kernel(pieces_ref, result_ref):
    result_ref[...] = sum_pieces(pieces_ref).astype(result_ref.dtype)


def gelu_kernel(pieces_ref, copies_ref, derivative_ref):
    total = sum_pieces(pieces_ref)
    hidden = derivative_ref.shape[1]
    values, derivative = gelu_pair(total[:, :hidden])
    derivative_ref[...] = derivative
    moved = (derivative * total[:, hidden:]).astype(copies_ref.dtype)
    active = values.astype(copies_ref.dtype)
    for n in range(copies_ref.shape[0]):
        copies_ref[n, :, :hidden] = moved
        copies_ref[n, :, hidden:] = active


def cotangent_kernel(pieces_ref, curvature_ref, curvature_far_ref, copies_ref):
    count, share, _ = pieces_ref.shape
    width = curvature_ref.shape[1]
    rows = pl.ds(pl.multiple_of(lax.axis_index("c") * share, share), share)
    total = sum_pieces(pieces_ref)
    own = (curvature_ref[rows, :] * total[:, :width]).astype(copies_ref.dtype)
    far = (curvature_far_ref[rows, :] * total[:, width:]).astype(copies_ref.dtype)
    for n in range(count):
        copies_ref[n, :, :width] = own
        copies_ref[n, :, width:] = far


def hidden_grad_kernel(pieces_ref, derivative_ref, copies_ref):
    grad = (sum_pieces(pieces_ref) * derivative_ref[...]).astype(copies_ref.dtype)
    for n in range(copies_ref.shape[0]):
        copies_ref[n] = grad


def apply_gelu(pieces, count, share):
    hidden = pieces.shape[1] // 2
    pieces = pieces.reshape(-1, share, 2 * hidden)
    results = [
        jax.ShapeDtypeStruct((count, share, 2 * hidden), jnp.bfloat16),
        jax.ShapeDtypeStruct((share, hidden), jnp.float32),
    ]
    copies, derivative = kernel_call(gelu_kernel, results, (pieces,), pieces.size)
    return copies.reshape(-1, 2 * hidden), derivative


def staged_then_direct(joined, share):
    pieces = exchange(joined, ("x",)).reshape(4, -1, joined.shape[1])
    results = [jax.ShapeDtypeStruct(pieces.shape[1:], jnp.bfloat16)]
    (partial,) = kernel_call(partial_sum_kernel, results, (pieces,), pieces.size)
    copies, derivative = apply_gelu(exchange(partial, ("zh",)), 16, share)
    return exchange(copies, ROWS), derivative


def direct_then_staged(joined, share):
    copies, derivative = apply_gelu(exchange(joined, ROWS), 4, share)
    block = exchange(copies, ("zh",))
    copies = jnp.broadcast_to(block[None], (4,) + block.shape).reshape(-1, block.shape[1])
    return exchange(copies, ("x",)), derivative


def swap_cores(block):
    return lax.ppermute(block, "c", SWAP)


def on_device(tokens, weight_in, tangent_in, weight_out, tangent_out, curvature):
    core = lax.axis_index("c")
    hidden = weight_in.shape[1]
    features = tokens.shape[1]
    share = tokens.shape[0] // 2

    halves = tokens.reshape(2, 1, share, features)
    copies = jnp.broadcast_to(halves, (2, lax.axis_size(TENSOR), share, features))
    arrived = exchange(copies.reshape(-1, features), ("c",) + TENSOR).reshape(2, -1, features)
    tokens_own = lax.dynamic_index_in_dim(arrived, core, 0, keepdims=False)
    tokens_far = lax.dynamic_index_in_dim(arrived, 1 - core, 0, keepdims=False)
    in_far, slope_far = swap_cores(weight_in), swap_cores(tangent_in)
    out_far, turn_far = swap_cores(weight_out), swap_cores(tangent_out)
    curvature_far = swap_cores(curvature)

    rows = arrived.shape[1]
    flops = 4 * rows * features * hidden
    preact, tangent = dot(tokens_own, weight_in), dot(tokens_own, tangent_in)
    (joined,) = kernel_call(
        far_products_kernel,
        [jax.ShapeDtypeStruct((rows, 2 * hidden), jnp.bfloat16)],
        (tokens_far, in_far, slope_far, preact, tangent),
        flops,
    )
    joined, out_far, turn_far, curvature_far = lax.optimization_barrier(
        (joined, out_far, turn_far, curvature_far)
    )
    both, derivative = lax.cond(
        core == 1,
        lambda j: staged_then_direct(j, share),
        lambda j: direct_then_staged(j, share),
        joined,
    )
    active = both[:, hidden:]

    (output_tangent,) = kernel_call(
        both_products_kernel,
        [jax.ShapeDtypeStruct((rows, 2 * features), jnp.bfloat16)],
        (both, weight_out, tangent_out, out_far, turn_far),
        2 * flops,
    )
    pieces = exchange(output_tangent, TENSOR).reshape(-1, share, 2 * features)
    (copies,) = kernel_call(
        cotangent_kernel,
        [jax.ShapeDtypeStruct(pieces.shape, jnp.bfloat16)],
        (pieces, curvature, curvature_far),
        pieces.size,
    )
    cotangent = exchange(copies.reshape(rows, 2 * features), TENSOR)
    cotangent_own, cotangent_far = cotangent[:, :features], cotangent[:, features:]

    backward = dot(cotangent_own, weight_out, 1, 1) + dot(cotangent_far, out_far, 1, 1)
    pieces = exchange(backward.astype(jnp.bfloat16), ROWS).reshape(-1, share, hidden)
    far_out = swap_cores(dot(active, cotangent_far, 0, 0).astype(jnp.bfloat16))
    product_out = dot(active, cotangent_own, 0, 0) + far_out.astype(jnp.float32)

    (copies,) = kernel_call(
        hidden_grad_kernel,
        [jax.ShapeDtypeStruct(pieces.shape, jnp.bfloat16)],
        (pieces, derivative),
        pieces.size,
    )
    hidden_grad = exchange(copies.reshape(rows, hidden), ROWS)
    product_out = product_out.astype(jnp.bfloat16)
    hidden_grad, product_out = lax.optimization_barrier((hidden_grad, product_out))
    far_in = swap_cores(dot(tokens_far, hidden_grad, 0, 0).astype(jnp.bfloat16))
    own_in = lax.optimization_barrier(dot(tokens_own, hidden_grad, 0, 0))
    product_in = (own_in + far_in.astype(jnp.float32)).astype(jnp.bfloat16)
    return (product_in, product_out)


def solution(mesh):
    fine = Mesh(mesh.devices.reshape(4, 4, 2, 8, 2), ("zh", "x", "c", "y", "zl"))
    by_dp = ("zh", "x", "c")
    return jax.shard_map(
        on_device,
        mesh=fine,
        in_specs=(
            P(TENSOR, by_dp),
            P(by_dp, TENSOR),
            P(by_dp, TENSOR),
            P(TENSOR, by_dp),
            P(TENSOR, by_dp),
            P(TENSOR, by_dp),
        ),
        out_specs=(P(by_dp, TENSOR), P(TENSOR, by_dp)),
        check_vma=False,
    )
```

```python
import math

import jax
import jax.numpy as jnp
from jax import lax
from jax.experimental import pallas as pl
from jax.experimental.pallas import tpu as pltpu
from jax.sharding import Mesh
from jax.sharding import PartitionSpec as P

gelu_scale = math.sqrt(2.0 / math.pi)
ROWS = ("x", "zh")
TENSOR = ("y", "zl")
SWAP = [(0, 1), (1, 0)]


def gelu_pair(hidden):
    argument = gelu_scale * (hidden + 0.044715 * hidden * hidden * hidden)
    hyper = jnp.tanh(argument)
    values = 0.5 * hidden * (1.0 + hyper)
    derivative = 0.5 * (1.0 + hyper) + 0.5 * hidden * (1.0 - hyper * hyper) * gelu_scale * (
        1.0 + 3.0 * 0.044715 * hidden * hidden
    )
    return (values, derivative)


def dot(left_side, right_side, left_dim=1, right_dim=0):
    return lax.dot_general(
        left_side,
        right_side,
        (((left_dim,), (right_dim,)), ((), ())),
        preferred_element_type=jnp.float32,
    )


def exchange(pieces, axes):
    return lax.all_to_all(pieces, axes, split_axis=0, concat_axis=0, tiled=True)


IN_VMEM = pl.BlockSpec(memory_space=pltpu.VMEM)


def kernel_call(kernel, results, operands, flops):
    moved_bytes = sum(x.size * x.dtype.itemsize for x in (*results, *operands))
    return pl.pallas_call(
        kernel,
        out_shape=results,
        in_specs=[IN_VMEM] * len(operands),
        out_specs=[IN_VMEM] * len(results),
        compiler_params=pltpu.CompilerParams(vmem_limit_bytes=16 * 2**20),
        cost_estimate=pl.CostEstimate(flops=flops, bytes_accessed=moved_bytes, transcendentals=0),
    )(*operands)


def far_products_kernel(far_ref, in_far_ref, slope_far_ref, preact_ref, tangent_ref, result_ref):
    hidden = in_far_ref.shape[1]
    far = far_ref[...]
    preact = preact_ref[...] + dot(far, in_far_ref[...])
    result_ref[:, :hidden] = preact.astype(result_ref.dtype)
    tangent = tangent_ref[...] + dot(far, slope_far_ref[...])
    result_ref[:, hidden:] = tangent.astype(result_ref.dtype)


def both_products_kernel(both_ref, out_ref, turn_ref, out_far_ref, turn_far_ref, result_ref):
    hidden, width = out_ref.shape
    moved, active = both_ref[:, :hidden], both_ref[:, hidden:]
    own = dot(moved, out_ref[...]) + dot(active, turn_ref[...])
    result_ref[:, :width] = own.astype(result_ref.dtype)
    far = dot(moved, out_far_ref[...]) + dot(active, turn_far_ref[...])
    result_ref[:, width:] = far.astype(result_ref.dtype)


def sum_pieces(pieces_ref):
    return jnp.sum(pieces_ref[...].astype(jnp.float32), axis=0)


def partial_sum_kernel(pieces_ref, result_ref):
    result_ref[...] = sum_pieces(pieces_ref).astype(result_ref.dtype)


def gelu_kernel(pieces_ref, copies_ref, derivative_ref):
    total = sum_pieces(pieces_ref)
    hidden = derivative_ref.shape[1]
    values, derivative = gelu_pair(total[:, :hidden])
    derivative_ref[...] = derivative
    moved = (derivative * total[:, hidden:]).astype(copies_ref.dtype)
    active = values.astype(copies_ref.dtype)
    for n in range(copies_ref.shape[0]):
        copies_ref[n, :, :hidden] = moved
        copies_ref[n, :, hidden:] = active


def cotangent_kernel(pieces_ref, curvature_ref, curvature_far_ref, copies_ref):
    count, share, _ = pieces_ref.shape
    width = curvature_ref.shape[1]
    rows = pl.ds(pl.multiple_of(lax.axis_index("c") * share, share), share)
    total = sum_pieces(pieces_ref)
    own = (curvature_ref[rows, :] * total[:, :width]).astype(copies_ref.dtype)
    far = (curvature_far_ref[rows, :] * total[:, width:]).astype(copies_ref.dtype)
    for n in range(count):
        copies_ref[n, :, :width] = own
        copies_ref[n, :, width:] = far


def hidden_grad_kernel(pieces_ref, derivative_ref, copies_ref):
    grad = (sum_pieces(pieces_ref) * derivative_ref[...]).astype(copies_ref.dtype)
    for n in range(copies_ref.shape[0]):
        copies_ref[n] = grad


def apply_gelu(pieces, count, share):
    hidden = pieces.shape[1] // 2
    pieces = pieces.reshape(-1, share, 2 * hidden)
    results = [
        jax.ShapeDtypeStruct((count, share, 2 * hidden), jnp.bfloat16),
        jax.ShapeDtypeStruct((share, hidden), jnp.float32),
    ]
    copies, derivative = kernel_call(gelu_kernel, results, (pieces,), pieces.size)
    return copies.reshape(-1, 2 * hidden), derivative


def staged_then_direct(joined, share):
    pieces = exchange(joined, ("x",)).reshape(4, -1, joined.shape[1])
    results = [jax.ShapeDtypeStruct(pieces.shape[1:], jnp.bfloat16)]
    (partial,) = kernel_call(partial_sum_kernel, results, (pieces,), pieces.size)
    copies, derivative = apply_gelu(exchange(partial, ("zh",)), 16, share)
    return exchange(copies, ROWS), derivative


def direct_then_staged(joined, share):
    copies, derivative = apply_gelu(exchange(joined, ROWS), 4, share)
    block = exchange(copies, ("zh",))
    copies = jnp.broadcast_to(block[None], (4,) + block.shape).reshape(-1, block.shape[1])
    return exchange(copies, ("x",)), derivative


def swap_cores(block):
    return lax.ppermute(block, "c", SWAP)


def on_device(tokens, weight_in, tangent_in, weight_out, tangent_out, curvature):
    core = lax.axis_index("c")
    hidden = weight_in.shape[1]
    features = tokens.shape[1]
    share = tokens.shape[0] // 2

    halves = tokens.reshape(2, 1, share, features)
    copies = jnp.broadcast_to(halves, (2, lax.axis_size(TENSOR), share, features))
    arrived = exchange(copies.reshape(-1, features), ("c",) + TENSOR).reshape(2, -1, features)
    tokens_own = lax.dynamic_index_in_dim(arrived, core, 0, keepdims=False)
    tokens_far = lax.dynamic_index_in_dim(arrived, 1 - core, 0, keepdims=False)
    in_far, slope_far = swap_cores(weight_in), swap_cores(tangent_in)
    out_far, turn_far = swap_cores(weight_out), swap_cores(tangent_out)
    curvature_far = swap_cores(curvature)

    rows = arrived.shape[1]
    flops = 4 * rows * features * hidden
    preact, tangent = dot(tokens_own, weight_in), dot(tokens_own, tangent_in)
    (joined,) = kernel_call(
        far_products_kernel,
        [jax.ShapeDtypeStruct((rows, 2 * hidden), jnp.bfloat16)],
        (tokens_far, in_far, slope_far, preact, tangent),
        flops,
    )
    joined, out_far, turn_far, curvature_far = lax.optimization_barrier(
        (joined, out_far, turn_far, curvature_far)
    )
    both, derivative = lax.cond(
        core != lax.axis_index("zl"),
        lambda j: staged_then_direct(j, share),
        lambda j: direct_then_staged(j, share),
        joined,
    )
    active = both[:, hidden:]

    (output_tangent,) = kernel_call(
        both_products_kernel,
        [jax.ShapeDtypeStruct((rows, 2 * features), jnp.bfloat16)],
        (both, weight_out, tangent_out, out_far, turn_far),
        2 * flops,
    )
    pieces = exchange(output_tangent, TENSOR).reshape(-1, share, 2 * features)
    (copies,) = kernel_call(
        cotangent_kernel,
        [jax.ShapeDtypeStruct(pieces.shape, jnp.bfloat16)],
        (pieces, curvature, curvature_far),
        pieces.size,
    )
    cotangent = exchange(copies.reshape(rows, 2 * features), TENSOR)
    cotangent_own, cotangent_far = cotangent[:, :features], cotangent[:, features:]

    backward = dot(cotangent_own, weight_out, 1, 1) + dot(cotangent_far, out_far, 1, 1)
    pieces = exchange(backward.astype(jnp.bfloat16), ROWS).reshape(-1, share, hidden)
    far_out = swap_cores(dot(active, cotangent_far, 0, 0).astype(jnp.bfloat16))
    product_out = dot(active, cotangent_own, 0, 0) + far_out.astype(jnp.float32)

    (copies,) = kernel_call(
        hidden_grad_kernel,
        [jax.ShapeDtypeStruct(pieces.shape, jnp.bfloat16)],
        (pieces, derivative),
        pieces.size,
    )
    hidden_grad = exchange(copies.reshape(rows, hidden), ROWS)
    product_out = product_out.astype(jnp.bfloat16)
    hidden_grad, product_out = lax.optimization_barrier((hidden_grad, product_out))
    far_in = swap_cores(dot(tokens_far, hidden_grad, 0, 0).astype(jnp.bfloat16))
    own_in = lax.optimization_barrier(dot(tokens_own, hidden_grad, 0, 0))
    product_in = (own_in + far_in.astype(jnp.float32)).astype(jnp.bfloat16)
    return (product_in, product_out)


def solution(mesh):
    fine = Mesh(mesh.devices.reshape(4, 4, 2, 8, 2), ("zh", "x", "c", "y", "zl"))
    by_dp = ("zh", "x", "c")
    return jax.shard_map(
        on_device,
        mesh=fine,
        in_specs=(
            P(TENSOR, by_dp),
            P(by_dp, TENSOR),
            P(by_dp, TENSOR),
            P(TENSOR, by_dp),
            P(TENSOR, by_dp),
            P(TENSOR, by_dp),
        ),
        out_specs=(P(by_dp, TENSOR), P(TENSOR, by_dp)),
        check_vma=False,
    )
```

```python
import math

import jax
import jax.numpy as jnp
from jax import lax
from jax.experimental import pallas as pl
from jax.experimental.pallas import tpu as pltpu
from jax.sharding import Mesh
from jax.sharding import PartitionSpec as P

gelu_scale = math.sqrt(2.0 / math.pi)
ROWS = ("x", "zh")
TENSOR = ("y", "zl")
SWAP = [(0, 1), (1, 0)]


def gelu_pair(hidden):
    argument = gelu_scale * (hidden + 0.044715 * hidden * hidden * hidden)
    hyper = jnp.tanh(argument)
    values = 0.5 * hidden * (1.0 + hyper)
    derivative = 0.5 * (1.0 + hyper) + 0.5 * hidden * (1.0 - hyper * hyper) * gelu_scale * (
        1.0 + 3.0 * 0.044715 * hidden * hidden
    )
    return (values, derivative)


def dot(left_side, right_side, left_dim=1, right_dim=0):
    return lax.dot_general(
        left_side,
        right_side,
        (((left_dim,), (right_dim,)), ((), ())),
        preferred_element_type=jnp.float32,
    )


def exchange(pieces, axes):
    return lax.all_to_all(pieces, axes, split_axis=0, concat_axis=0, tiled=True)


IN_VMEM = pl.BlockSpec(memory_space=pltpu.VMEM)


def kernel_call(kernel, results, operands, flops):
    moved_bytes = sum(x.size * x.dtype.itemsize for x in (*results, *operands))
    return pl.pallas_call(
        kernel,
        out_shape=results,
        in_specs=[IN_VMEM] * len(operands),
        out_specs=[IN_VMEM] * len(results),
        compiler_params=pltpu.CompilerParams(vmem_limit_bytes=8 * 2**20),
        cost_estimate=pl.CostEstimate(flops=flops, bytes_accessed=moved_bytes, transcendentals=0),
    )(*operands)


def far_products_kernel(far_ref, in_far_ref, slope_far_ref, preact_ref, tangent_ref, result_ref):
    hidden = in_far_ref.shape[1]
    far = far_ref[...]
    preact = preact_ref[...] + dot(far, in_far_ref[...])
    result_ref[:, :hidden] = preact.astype(result_ref.dtype)
    tangent = tangent_ref[...] + dot(far, slope_far_ref[...])
    result_ref[:, hidden:] = tangent.astype(result_ref.dtype)


def both_products_kernel(both_ref, out_ref, turn_ref, out_far_ref, turn_far_ref, result_ref):
    hidden, width = out_ref.shape
    moved, active = both_ref[:, :hidden], both_ref[:, hidden:]
    own = dot(moved, out_ref[...]) + dot(active, turn_ref[...])
    result_ref[:, :width] = own.astype(result_ref.dtype)
    far = dot(moved, out_far_ref[...]) + dot(active, turn_far_ref[...])
    result_ref[:, width:] = far.astype(result_ref.dtype)


def backward_kernel(cotangent_ref, out_ref, out_far_ref, result_ref):
    width = out_ref.shape[1]
    total = dot(cotangent_ref[:, :width], out_ref[...], 1, 1)
    total += dot(cotangent_ref[:, width:], out_far_ref[...], 1, 1)
    result_ref[...] = total.astype(result_ref.dtype)


def sum_pieces(pieces_ref):
    return jnp.sum(pieces_ref[...].astype(jnp.float32), axis=0)


def partial_sum_kernel(pieces_ref, result_ref):
    result_ref[...] = sum_pieces(pieces_ref).astype(result_ref.dtype)


def gelu_kernel(pieces_ref, copies_ref, derivative_ref):
    total = sum_pieces(pieces_ref)
    hidden = derivative_ref.shape[1]
    values, derivative = gelu_pair(total[:, :hidden])
    derivative_ref[...] = derivative
    moved = (derivative * total[:, hidden:]).astype(copies_ref.dtype)
    active = values.astype(copies_ref.dtype)
    for n in range(copies_ref.shape[0]):
        copies_ref[n, :, :hidden] = moved
        copies_ref[n, :, hidden:] = active


def cotangent_kernel(pieces_ref, curvature_ref, curvature_far_ref, copies_ref):
    count, share, _ = pieces_ref.shape
    width = curvature_ref.shape[1]
    rows = pl.ds(pl.multiple_of(lax.axis_index("c") * share, share), share)
    total = sum_pieces(pieces_ref)
    own = (curvature_ref[rows, :] * total[:, :width]).astype(copies_ref.dtype)
    far = (curvature_far_ref[rows, :] * total[:, width:]).astype(copies_ref.dtype)
    for n in range(count):
        copies_ref[n, :, :width] = own
        copies_ref[n, :, width:] = far


def hidden_grad_kernel(pieces_ref, derivative_ref, copies_ref):
    grad = (sum_pieces(pieces_ref) * derivative_ref[...]).astype(copies_ref.dtype)
    for n in range(copies_ref.shape[0]):
        copies_ref[n] = grad


def apply_gelu(pieces, count, share):
    hidden = pieces.shape[1] // 2
    pieces = pieces.reshape(-1, share, 2 * hidden)
    results = [
        jax.ShapeDtypeStruct((count, share, 2 * hidden), jnp.bfloat16),
        jax.ShapeDtypeStruct((share, hidden), jnp.float32),
    ]
    copies, derivative = kernel_call(gelu_kernel, results, (pieces,), pieces.size)
    return copies.reshape(-1, 2 * hidden), derivative


def staged_then_direct(joined, share):
    pieces = exchange(joined, ("x",)).reshape(4, -1, joined.shape[1])
    results = [jax.ShapeDtypeStruct(pieces.shape[1:], jnp.bfloat16)]
    (partial,) = kernel_call(partial_sum_kernel, results, (pieces,), pieces.size)
    copies, derivative = apply_gelu(exchange(partial, ("zh",)), 16, share)
    return exchange(copies, ROWS), derivative


def direct_then_staged(joined, share):
    copies, derivative = apply_gelu(exchange(joined, ROWS), 4, share)
    block = exchange(copies, ("zh",))
    copies = jnp.broadcast_to(block[None], (4,) + block.shape).reshape(-1, block.shape[1])
    return exchange(copies, ("x",)), derivative


def swap_cores(block):
    return lax.ppermute(block, "c", SWAP)


def on_device(tokens, weight_in, tangent_in, weight_out, tangent_out, curvature):
    core = lax.axis_index("c")
    hidden = weight_in.shape[1]
    features = tokens.shape[1]
    share = tokens.shape[0] // 2

    halves = tokens.reshape(2, 1, share, features)
    copies = jnp.broadcast_to(halves, (2, lax.axis_size(TENSOR), share, features))
    arrived = exchange(copies.reshape(-1, features), ("c",) + TENSOR).reshape(2, -1, features)
    tokens_own = lax.dynamic_index_in_dim(arrived, core, 0, keepdims=False)
    tokens_far = lax.dynamic_index_in_dim(arrived, 1 - core, 0, keepdims=False)
    in_far, slope_far = swap_cores(weight_in), swap_cores(tangent_in)
    out_far, turn_far = swap_cores(weight_out), swap_cores(tangent_out)
    curvature_far = swap_cores(curvature)

    rows = arrived.shape[1]
    flops = 4 * rows * features * hidden
    preact, tangent = dot(tokens_own, weight_in), dot(tokens_own, tangent_in)
    (joined,) = kernel_call(
        far_products_kernel,
        [jax.ShapeDtypeStruct((rows, 2 * hidden), jnp.bfloat16)],
        (tokens_far, in_far, slope_far, preact, tangent),
        flops,
    )
    joined, out_far, turn_far, curvature_far = lax.optimization_barrier(
        (joined, out_far, turn_far, curvature_far)
    )
    both, derivative = lax.cond(
        core != lax.axis_index("zl"),
        lambda j: staged_then_direct(j, share),
        lambda j: direct_then_staged(j, share),
        joined,
    )
    active = both[:, hidden:]

    (output_tangent,) = kernel_call(
        both_products_kernel,
        [jax.ShapeDtypeStruct((rows, 2 * features), jnp.bfloat16)],
        (both, weight_out, tangent_out, out_far, turn_far),
        2 * flops,
    )
    pieces = exchange(output_tangent, TENSOR).reshape(-1, share, 2 * features)
    (copies,) = kernel_call(
        cotangent_kernel,
        [jax.ShapeDtypeStruct(pieces.shape, jnp.bfloat16)],
        (pieces, curvature, curvature_far),
        pieces.size,
    )
    cotangent = exchange(copies.reshape(rows, 2 * features), TENSOR)
    cotangent_own, cotangent_far = cotangent[:, :features], cotangent[:, features:]

    (backward,) = kernel_call(
        backward_kernel,
        [jax.ShapeDtypeStruct((rows, hidden), jnp.bfloat16)],
        (cotangent, weight_out, out_far),
        flops,
    )
    pieces = exchange(backward, ROWS).reshape(-1, share, hidden)
    far_out = swap_cores(dot(active, cotangent_far, 0, 0).astype(jnp.bfloat16))
    product_out = dot(active, cotangent_own, 0, 0) + far_out.astype(jnp.float32)

    (copies,) = kernel_call(
        hidden_grad_kernel,
        [jax.ShapeDtypeStruct(pieces.shape, jnp.bfloat16)],
        (pieces, derivative),
        pieces.size,
    )
    hidden_grad = exchange(copies.reshape(rows, hidden), ROWS)
    product_out = product_out.astype(jnp.bfloat16)
    hidden_grad, product_out = lax.optimization_barrier((hidden_grad, product_out))
    far_in = swap_cores(dot(tokens_far, hidden_grad, 0, 0).astype(jnp.bfloat16))
    own_in = lax.optimization_barrier(dot(tokens_own, hidden_grad, 0, 0))
    product_in = (own_in + far_in.astype(jnp.float32)).astype(jnp.bfloat16)
    return (product_in, product_out)


def solution(mesh):
    fine = Mesh(mesh.devices.reshape(4, 4, 2, 8, 2), ("zh", "x", "c", "y", "zl"))
    by_dp = ("zh", "x", "c")
    return jax.shard_map(
        on_device,
        mesh=fine,
        in_specs=(
            P(TENSOR, by_dp),
            P(by_dp, TENSOR),
            P(by_dp, TENSOR),
            P(TENSOR, by_dp),
            P(TENSOR, by_dp),
            P(TENSOR, by_dp),
        ),
        out_specs=(P(by_dp, TENSOR), P(TENSOR, by_dp)),
        check_vma=False,
    )
```

```python
import math

import jax
import jax.numpy as jnp
from jax import lax
from jax.experimental import pallas as pl
from jax.experimental.pallas import tpu as pltpu
from jax.sharding import Mesh
from jax.sharding import PartitionSpec as P

gelu_scale = math.sqrt(2.0 / math.pi)
ROWS = ("x", "zh")
TENSOR = ("y", "zl")
SWAP = [(0, 1), (1, 0)]


def gelu_pair(hidden):
    argument = gelu_scale * (hidden + 0.044715 * hidden * hidden * hidden)
    hyper = jnp.tanh(argument)
    values = 0.5 * hidden * (1.0 + hyper)
    derivative = 0.5 * (1.0 + hyper) + 0.5 * hidden * (1.0 - hyper * hyper) * gelu_scale * (
        1.0 + 3.0 * 0.044715 * hidden * hidden
    )
    return (values, derivative)


def dot(left_side, right_side, left_dim=1, right_dim=0):
    return lax.dot_general(
        left_side,
        right_side,
        (((left_dim,), (right_dim,)), ((), ())),
        preferred_element_type=jnp.float32,
    )


def exchange(pieces, axes):
    return lax.all_to_all(pieces, axes, split_axis=0, concat_axis=0, tiled=True)


IN_VMEM = pl.BlockSpec(memory_space=pltpu.VMEM)


def kernel_call(kernel, results, operands, flops):
    moved_bytes = sum(x.size * x.dtype.itemsize for x in (*results, *operands))
    return pl.pallas_call(
        kernel,
        out_shape=results,
        in_specs=[IN_VMEM] * len(operands),
        out_specs=[IN_VMEM] * len(results),
        compiler_params=pltpu.CompilerParams(vmem_limit_bytes=8 * 2**20),
        cost_estimate=pl.CostEstimate(flops=flops, bytes_accessed=moved_bytes, transcendentals=0),
    )(*operands)


def far_products_kernel(far_ref, in_far_ref, slope_far_ref, preact_ref, tangent_ref, result_ref):
    hidden = in_far_ref.shape[1]
    far = far_ref[...]
    preact = preact_ref[...] + dot(far, in_far_ref[...])
    result_ref[:, :hidden] = preact.astype(result_ref.dtype)
    tangent = tangent_ref[...] + dot(far, slope_far_ref[...])
    result_ref[:, hidden:] = tangent.astype(result_ref.dtype)


def both_products_kernel(both_ref, out_ref, turn_ref, out_far_ref, turn_far_ref, result_ref):
    hidden, width = out_ref.shape
    moved, active = both_ref[:, :hidden], both_ref[:, hidden:]
    own = dot(moved, out_ref[...]) + dot(active, turn_ref[...])
    result_ref[:, :width] = own.astype(result_ref.dtype)
    far = dot(moved, out_far_ref[...]) + dot(active, turn_far_ref[...])
    result_ref[:, width:] = far.astype(result_ref.dtype)


def backward_kernel(cotangent_ref, out_ref, out_far_ref, result_ref):
    width = out_ref.shape[1]
    total = dot(cotangent_ref[:, :width], out_ref[...], 1, 1)
    total += dot(cotangent_ref[:, width:], out_far_ref[...], 1, 1)
    result_ref[...] = total.astype(result_ref.dtype)


def sum_pieces(pieces_ref):
    return jnp.sum(pieces_ref[...].astype(jnp.float32), axis=0)


def partial_sum_kernel(pieces_ref, result_ref):
    result_ref[...] = sum_pieces(pieces_ref).astype(result_ref.dtype)


def copies_kernel(halves_ref, copies_ref):
    for n in range(copies_ref.shape[1]):
        copies_ref[:, n] = halves_ref[...]


def gelu_kernel(pieces_ref, copies_ref, derivative_ref):
    total = sum_pieces(pieces_ref)
    hidden = derivative_ref.shape[1]
    values, derivative = gelu_pair(total[:, :hidden])
    derivative_ref[...] = derivative
    moved = (derivative * total[:, hidden:]).astype(copies_ref.dtype)
    active = values.astype(copies_ref.dtype)
    for n in range(copies_ref.shape[0]):
        copies_ref[n, :, :hidden] = moved
        copies_ref[n, :, hidden:] = active


def cotangent_kernel(pieces_ref, curvature_ref, curvature_far_ref, copies_ref):
    count, share, _ = pieces_ref.shape
    width = curvature_ref.shape[1]
    rows = pl.ds(pl.multiple_of(lax.axis_index("c") * share, share), share)
    total = sum_pieces(pieces_ref)
    own = (curvature_ref[rows, :] * total[:, :width]).astype(copies_ref.dtype)
    far = (curvature_far_ref[rows, :] * total[:, width:]).astype(copies_ref.dtype)
    for n in range(count):
        copies_ref[n, :, :width] = own
        copies_ref[n, :, width:] = far


def hidden_grad_kernel(pieces_ref, derivative_ref, copies_ref):
    grad = (sum_pieces(pieces_ref) * derivative_ref[...]).astype(copies_ref.dtype)
    for n in range(copies_ref.shape[0]):
        copies_ref[n] = grad


def apply_gelu(pieces, count, share):
    hidden = pieces.shape[1] // 2
    pieces = pieces.reshape(-1, share, 2 * hidden)
    results = [
        jax.ShapeDtypeStruct((count, share, 2 * hidden), jnp.bfloat16),
        jax.ShapeDtypeStruct((share, hidden), jnp.float32),
    ]
    copies, derivative = kernel_call(gelu_kernel, results, (pieces,), pieces.size)
    return copies.reshape(-1, 2 * hidden), derivative


def staged_then_direct(joined, share):
    pieces = exchange(joined, ("x",)).reshape(4, -1, joined.shape[1])
    results = [jax.ShapeDtypeStruct(pieces.shape[1:], jnp.bfloat16)]
    (partial,) = kernel_call(partial_sum_kernel, results, (pieces,), pieces.size)
    copies, derivative = apply_gelu(exchange(partial, ("zh",)), 16, share)
    return exchange(copies, ROWS), derivative


def direct_then_staged(joined, share):
    copies, derivative = apply_gelu(exchange(joined, ROWS), 4, share)
    block = exchange(copies, ("zh",))
    copies = jnp.broadcast_to(block[None], (4,) + block.shape).reshape(-1, block.shape[1])
    return exchange(copies, ("x",)), derivative


def swap_cores(block):
    return lax.ppermute(block, "c", SWAP)


def on_device(tokens, weight_in, tangent_in, weight_out, tangent_out, curvature):
    core = lax.axis_index("c")
    hidden = weight_in.shape[1]
    features = tokens.shape[1]
    share = tokens.shape[0] // 2

    halves = tokens.reshape(2, share, features)
    shape = (2, lax.axis_size(TENSOR), share, features)
    (copies,) = kernel_call(
        copies_kernel, [jax.ShapeDtypeStruct(shape, tokens.dtype)], (halves,), 0
    )
    arrived = exchange(copies.reshape(-1, features), ("c",) + TENSOR).reshape(2, -1, features)
    tokens_own = lax.dynamic_index_in_dim(arrived, core, 0, keepdims=False)
    tokens_far = lax.dynamic_index_in_dim(arrived, 1 - core, 0, keepdims=False)
    in_far, slope_far = swap_cores(weight_in), swap_cores(tangent_in)
    out_far, turn_far = swap_cores(weight_out), swap_cores(tangent_out)
    curvature_far = swap_cores(curvature)

    rows = arrived.shape[1]
    flops = 4 * rows * features * hidden
    preact, tangent = dot(tokens_own, weight_in), dot(tokens_own, tangent_in)
    (joined,) = kernel_call(
        far_products_kernel,
        [jax.ShapeDtypeStruct((rows, 2 * hidden), jnp.bfloat16)],
        (tokens_far, in_far, slope_far, preact, tangent),
        flops,
    )
    joined, out_far, turn_far, curvature_far = lax.optimization_barrier(
        (joined, out_far, turn_far, curvature_far)
    )
    both, derivative = lax.cond(
        core != lax.axis_index("zl"),
        lambda j: staged_then_direct(j, share),
        lambda j: direct_then_staged(j, share),
        joined,
    )
    active = both[:, hidden:]

    (output_tangent,) = kernel_call(
        both_products_kernel,
        [jax.ShapeDtypeStruct((rows, 2 * features), jnp.bfloat16)],
        (both, weight_out, tangent_out, out_far, turn_far),
        2 * flops,
    )
    pieces = exchange(output_tangent, TENSOR).reshape(-1, share, 2 * features)
    (copies,) = kernel_call(
        cotangent_kernel,
        [jax.ShapeDtypeStruct(pieces.shape, jnp.bfloat16)],
        (pieces, curvature, curvature_far),
        pieces.size,
    )
    cotangent = exchange(copies.reshape(rows, 2 * features), TENSOR)
    cotangent_own, cotangent_far = cotangent[:, :features], cotangent[:, features:]

    (backward,) = kernel_call(
        backward_kernel,
        [jax.ShapeDtypeStruct((rows, hidden), jnp.bfloat16)],
        (cotangent, weight_out, out_far),
        flops,
    )
    pieces = exchange(backward, ROWS).reshape(-1, share, hidden)
    far_out = swap_cores(dot(active, cotangent_far, 0, 0).astype(jnp.bfloat16))
    product_out = dot(active, cotangent_own, 0, 0) + far_out.astype(jnp.float32)

    (copies,) = kernel_call(
        hidden_grad_kernel,
        [jax.ShapeDtypeStruct(pieces.shape, jnp.bfloat16)],
        (pieces, derivative),
        pieces.size,
    )
    hidden_grad = exchange(copies.reshape(rows, hidden), ROWS)
    product_out = product_out.astype(jnp.bfloat16)
    hidden_grad, product_out = lax.optimization_barrier((hidden_grad, product_out))
    far_in = swap_cores(dot(tokens_far, hidden_grad, 0, 0).astype(jnp.bfloat16))
    own_in = lax.optimization_barrier(dot(tokens_own, hidden_grad, 0, 0))
    product_in = (own_in + far_in.astype(jnp.float32)).astype(jnp.bfloat16)
    return (product_in, product_out)


def solution(mesh):
    fine = Mesh(mesh.devices.reshape(4, 4, 2, 8, 2), ("zh", "x", "c", "y", "zl"))
    by_dp = ("zh", "x", "c")
    return jax.shard_map(
        on_device,
        mesh=fine,
        in_specs=(
            P(TENSOR, by_dp),
            P(by_dp, TENSOR),
            P(by_dp, TENSOR),
            P(TENSOR, by_dp),
            P(TENSOR, by_dp),
            P(TENSOR, by_dp),
        ),
        out_specs=(P(by_dp, TENSOR), P(TENSOR, by_dp)),
        check_vma=False,
    )
```

```python
import math

import jax
import jax.numpy as jnp
from jax import lax
from jax.experimental import pallas as pl
from jax.experimental.pallas import tpu as pltpu
from jax.sharding import Mesh
from jax.sharding import PartitionSpec as P

gelu_scale = math.sqrt(2.0 / math.pi)
ROWS = ("x", "zh")
TENSOR = ("y", "zl")
SWAP = [(0, 1), (1, 0)]


def gelu_pair(hidden):
    argument = gelu_scale * (hidden + 0.044715 * hidden * hidden * hidden)
    hyper = jnp.tanh(argument)
    values = 0.5 * hidden * (1.0 + hyper)
    derivative = 0.5 * (1.0 + hyper) + 0.5 * hidden * (1.0 - hyper * hyper) * gelu_scale * (
        1.0 + 3.0 * 0.044715 * hidden * hidden
    )
    return (values, derivative)


def dot(left_side, right_side, left_dim=1, right_dim=0):
    return lax.dot_general(
        left_side,
        right_side,
        (((left_dim,), (right_dim,)), ((), ())),
        preferred_element_type=jnp.float32,
    )


def exchange(pieces, axes):
    return lax.all_to_all(pieces, axes, split_axis=0, concat_axis=0, tiled=True)


IN_VMEM = pl.BlockSpec(memory_space=pltpu.VMEM)


def kernel_call(kernel, results, operands, flops):
    moved_bytes = sum(x.size * x.dtype.itemsize for x in (*results, *operands))
    return pl.pallas_call(
        kernel,
        out_shape=results,
        in_specs=[IN_VMEM] * len(operands),
        out_specs=[IN_VMEM] * len(results),
        compiler_params=pltpu.CompilerParams(vmem_limit_bytes=8 * 2**20),
        cost_estimate=pl.CostEstimate(flops=flops, bytes_accessed=moved_bytes, transcendentals=0),
    )(*operands)


def far_products_kernel(far_ref, in_far_ref, slope_far_ref, preact_ref, tangent_ref, result_ref):
    hidden = in_far_ref.shape[1]
    far = far_ref[...]
    preact = preact_ref[...] + dot(far, in_far_ref[...])
    result_ref[:, :hidden] = preact.astype(result_ref.dtype)
    tangent = tangent_ref[...] + dot(far, slope_far_ref[...])
    result_ref[:, hidden:] = tangent.astype(result_ref.dtype)


def both_products_kernel(both_ref, out_ref, turn_ref, out_far_ref, turn_far_ref, result_ref):
    hidden, width = out_ref.shape
    moved, active = both_ref[:, :hidden], both_ref[:, hidden:]
    own = dot(moved, out_ref[...]) + dot(active, turn_ref[...])
    result_ref[:, :width] = own.astype(result_ref.dtype)
    far = dot(moved, out_far_ref[...]) + dot(active, turn_far_ref[...])
    result_ref[:, width:] = far.astype(result_ref.dtype)


def backward_kernel(cotangent_ref, out_ref, out_far_ref, result_ref):
    width = out_ref.shape[1]
    total = dot(cotangent_ref[:, :width], out_ref[...], 1, 1)
    total += dot(cotangent_ref[:, width:], out_far_ref[...], 1, 1)
    result_ref[...] = total.astype(result_ref.dtype)


def sum_pieces(pieces_ref):
    return jnp.sum(pieces_ref[...].astype(jnp.float32), axis=0)


def partial_sum_kernel(pieces_ref, result_ref):
    result_ref[...] = sum_pieces(pieces_ref).astype(result_ref.dtype)


def gelu_kernel(pieces_ref, copies_ref, derivative_ref):
    total = sum_pieces(pieces_ref)
    hidden = derivative_ref.shape[1]
    values, derivative = gelu_pair(total[:, :hidden])
    derivative_ref[...] = derivative
    moved = (derivative * total[:, hidden:]).astype(copies_ref.dtype)
    active = values.astype(copies_ref.dtype)
    for n in range(copies_ref.shape[0]):
        copies_ref[n, :, :hidden] = moved
        copies_ref[n, :, hidden:] = active


def cotangent_kernel(pieces_ref, curvature_ref, curvature_far_ref, copies_ref):
    count, share, _ = pieces_ref.shape
    width = curvature_ref.shape[1]
    rows = pl.ds(pl.multiple_of(lax.axis_index("c") * share, share), share)
    total = sum_pieces(pieces_ref)
    own = (curvature_ref[rows, :] * total[:, :width]).astype(copies_ref.dtype)
    far = (curvature_far_ref[rows, :] * total[:, width:]).astype(copies_ref.dtype)
    for n in range(count):
        copies_ref[n, :, :width] = own
        copies_ref[n, :, width:] = far


def hidden_grad_kernel(pieces_ref, derivative_ref, copies_ref):
    grad = (sum_pieces(pieces_ref) * derivative_ref[...]).astype(copies_ref.dtype)
    for n in range(copies_ref.shape[0]):
        copies_ref[n] = grad


def apply_gelu(pieces, count, share):
    hidden = pieces.shape[1] // 2
    pieces = pieces.reshape(-1, share, 2 * hidden)
    results = [
        jax.ShapeDtypeStruct((count, share, 2 * hidden), jnp.bfloat16),
        jax.ShapeDtypeStruct((share, hidden), jnp.float32),
    ]
    copies, derivative = kernel_call(gelu_kernel, results, (pieces,), pieces.size)
    return copies.reshape(-1, 2 * hidden), derivative


def staged_then_direct(joined, share):
    pieces = exchange(joined, ("x",)).reshape(4, -1, joined.shape[1])
    results = [jax.ShapeDtypeStruct(pieces.shape[1:], jnp.bfloat16)]
    (partial,) = kernel_call(partial_sum_kernel, results, (pieces,), pieces.size)
    copies, derivative = apply_gelu(exchange(partial, ("zh",)), 16, share)
    return exchange(copies, ROWS), derivative


def direct_then_staged(joined, share):
    copies, derivative = apply_gelu(exchange(joined, ROWS), 4, share)
    block = exchange(copies, ("zh",))
    copies = jnp.broadcast_to(block[None], (4,) + block.shape).reshape(-1, block.shape[1])
    return exchange(copies, ("x",)), derivative


def swap_cores(block):
    return lax.ppermute(block, "c", SWAP)


def on_device(tokens, weight_in, tangent_in, weight_out, tangent_out, curvature):
    core = lax.axis_index("c")
    hidden = weight_in.shape[1]
    features = tokens.shape[1]
    share = tokens.shape[0] // 2

    halves = tokens.reshape(2, 1, share, features)
    copies = jnp.broadcast_to(halves, (2, lax.axis_size(TENSOR), share, features))
    arrived = exchange(copies.reshape(-1, features), ("c",) + TENSOR).reshape(2, -1, features)
    tokens_own = lax.dynamic_index_in_dim(arrived, core, 0, keepdims=False)
    tokens_far = lax.dynamic_index_in_dim(arrived, 1 - core, 0, keepdims=False)
    in_far, slope_far = swap_cores(weight_in), swap_cores(tangent_in)
    out_far, turn_far = swap_cores(weight_out), swap_cores(tangent_out)
    curvature_far = swap_cores(curvature)

    rows = arrived.shape[1]
    flops = 4 * rows * features * hidden
    preact, tangent = dot(tokens_own, weight_in), dot(tokens_own, tangent_in)
    (joined,) = kernel_call(
        far_products_kernel,
        [jax.ShapeDtypeStruct((rows, 2 * hidden), jnp.bfloat16)],
        (tokens_far, in_far, slope_far, preact, tangent),
        flops,
    )
    joined, out_far, turn_far, curvature_far = lax.optimization_barrier(
        (joined, out_far, turn_far, curvature_far)
    )
    both, derivative = lax.cond(
        core != lax.axis_index("zl"),
        lambda j: staged_then_direct(j, share),
        lambda j: direct_then_staged(j, share),
        joined,
    )
    active = both[:, hidden:]

    (output_tangent,) = kernel_call(
        both_products_kernel,
        [jax.ShapeDtypeStruct((rows, 2 * features), jnp.bfloat16)],
        (both, weight_out, tangent_out, out_far, turn_far),
        2 * flops,
    )
    pieces = exchange(output_tangent, TENSOR).reshape(-1, share, 2 * features)
    (copies,) = kernel_call(
        cotangent_kernel,
        [jax.ShapeDtypeStruct(pieces.shape, jnp.bfloat16)],
        (pieces, curvature, curvature_far),
        pieces.size,
    )
    cotangent = exchange(copies.reshape(rows, 2 * features), TENSOR)
    cotangent_own, cotangent_far = cotangent[:, :features], cotangent[:, features:]

    (backward,) = kernel_call(
        backward_kernel,
        [jax.ShapeDtypeStruct((rows, hidden), jnp.bfloat16)],
        (cotangent, weight_out, out_far),
        flops,
    )
    pieces = exchange(backward, ROWS).reshape(-1, share, hidden)
    far_out = swap_cores(dot(active, cotangent_far, 0, 0).astype(jnp.bfloat16))
    product_out = dot(active, cotangent_own, 0, 0) + far_out.astype(jnp.float32)

    (copies,) = kernel_call(
        hidden_grad_kernel,
        [jax.ShapeDtypeStruct(pieces.shape, jnp.bfloat16)],
        (pieces, derivative),
        pieces.size,
    )
    hidden_grad = exchange(copies.reshape(rows, hidden), ROWS)
    product_out = product_out.astype(jnp.bfloat16)
    sent, far_out = lax.optimization_barrier((tokens_far, far_out))
    tokens_cross = swap_cores(sent)
    hidden_grad, product_out, tokens_cross = lax.optimization_barrier(
        (hidden_grad, product_out, tokens_cross)
    )
    far_grad = swap_cores(hidden_grad)
    own_in = lax.optimization_barrier(dot(tokens_own, hidden_grad, 0, 0))
    product_in = (own_in + dot(tokens_cross, far_grad, 0, 0)).astype(jnp.bfloat16)
    return (product_in, product_out)


def solution(mesh):
    fine = Mesh(mesh.devices.reshape(4, 4, 2, 8, 2), ("zh", "x", "c", "y", "zl"))
    by_dp = ("zh", "x", "c")
    return jax.shard_map(
        on_device,
        mesh=fine,
        in_specs=(
            P(TENSOR, by_dp),
            P(by_dp, TENSOR),
            P(by_dp, TENSOR),
            P(TENSOR, by_dp),
            P(TENSOR, by_dp),
            P(TENSOR, by_dp),
        ),
        out_specs=(P(by_dp, TENSOR), P(TENSOR, by_dp)),
        check_vma=False,
    )
```

```python
import math

import jax
import jax.numpy as jnp
from jax import lax
from jax.experimental import pallas as pl
from jax.experimental.pallas import tpu as pltpu
from jax.sharding import Mesh
from jax.sharding import PartitionSpec as P

gelu_scale = math.sqrt(2.0 / math.pi)
ROWS = ("x", "zh")
TENSOR = ("y", "zl")
SWAP = [(0, 1), (1, 0)]


def gelu_pair(hidden):
    argument = gelu_scale * (hidden + 0.044715 * hidden * hidden * hidden)
    hyper = jnp.tanh(argument)
    values = 0.5 * hidden * (1.0 + hyper)
    derivative = 0.5 * (1.0 + hyper) + 0.5 * hidden * (1.0 - hyper * hyper) * gelu_scale * (
        1.0 + 3.0 * 0.044715 * hidden * hidden
    )
    return (values, derivative)


def dot(left_side, right_side, left_dim=1, right_dim=0):
    return lax.dot_general(
        left_side,
        right_side,
        (((left_dim,), (right_dim,)), ((), ())),
        preferred_element_type=jnp.float32,
    )


def exchange(pieces, axes):
    return lax.all_to_all(pieces, axes, split_axis=0, concat_axis=0, tiled=True)


IN_VMEM = pl.BlockSpec(memory_space=pltpu.VMEM)


def kernel_call(kernel, results, operands, flops):
    moved_bytes = sum(x.size * x.dtype.itemsize for x in (*results, *operands))
    return pl.pallas_call(
        kernel,
        out_shape=results,
        in_specs=[IN_VMEM] * len(operands),
        out_specs=[IN_VMEM] * len(results),
        compiler_params=pltpu.CompilerParams(vmem_limit_bytes=8 * 2**20),
        cost_estimate=pl.CostEstimate(flops=flops, bytes_accessed=moved_bytes, transcendentals=0),
    )(*operands)


def far_products_kernel(far_ref, in_far_ref, slope_far_ref, preact_ref, tangent_ref, result_ref):
    hidden = in_far_ref.shape[1]
    far = far_ref[...]
    preact = preact_ref[...] + dot(far, in_far_ref[...])
    result_ref[:, :hidden] = preact.astype(result_ref.dtype)
    tangent = tangent_ref[...] + dot(far, slope_far_ref[...])
    result_ref[:, hidden:] = tangent.astype(result_ref.dtype)


def both_products_kernel(both_ref, out_ref, turn_ref, out_far_ref, turn_far_ref, result_ref):
    hidden, width = out_ref.shape
    moved, active = both_ref[:, :hidden], both_ref[:, hidden:]
    own = dot(moved, out_ref[...]) + dot(active, turn_ref[...])
    result_ref[:, :width] = own.astype(result_ref.dtype)
    far = dot(moved, out_far_ref[...]) + dot(active, turn_far_ref[...])
    result_ref[:, width:] = far.astype(result_ref.dtype)


def backward_kernel(cotangent_ref, out_ref, out_far_ref, result_ref):
    width = out_ref.shape[1]
    total = dot(cotangent_ref[:, :width], out_ref[...], 1, 1)
    total += dot(cotangent_ref[:, width:], out_far_ref[...], 1, 1)
    result_ref[...] = total.astype(result_ref.dtype)


def sum_pieces(pieces_ref):
    return jnp.sum(pieces_ref[...].astype(jnp.float32), axis=0)


def partial_sum_kernel(pieces_ref, result_ref):
    result_ref[...] = sum_pieces(pieces_ref).astype(result_ref.dtype)


def gelu_kernel(pieces_ref, copies_ref, derivative_ref):
    total = sum_pieces(pieces_ref)
    hidden = derivative_ref.shape[1]
    values, derivative = gelu_pair(total[:, :hidden])
    derivative_ref[...] = derivative
    moved = (derivative * total[:, hidden:]).astype(copies_ref.dtype)
    active = values.astype(copies_ref.dtype)
    for n in range(copies_ref.shape[0]):
        copies_ref[n, :, :hidden] = moved
        copies_ref[n, :, hidden:] = active


def cotangent_kernel(pieces_ref, curvature_ref, curvature_far_ref, copies_ref):
    count, share, _ = pieces_ref.shape
    width = curvature_ref.shape[1]
    rows = pl.ds(pl.multiple_of(lax.axis_index("c") * share, share), share)
    total = sum_pieces(pieces_ref)
    own = (curvature_ref[rows, :] * total[:, :width]).astype(copies_ref.dtype)
    far = (curvature_far_ref[rows, :] * total[:, width:]).astype(copies_ref.dtype)
    for n in range(count):
        copies_ref[n, :, :width] = own
        copies_ref[n, :, width:] = far


def hidden_grad_kernel(pieces_ref, derivative_ref, copies_ref):
    grad = (sum_pieces(pieces_ref) * derivative_ref[...]).astype(copies_ref.dtype)
    for n in range(copies_ref.shape[0]):
        copies_ref[n] = grad


def apply_gelu(pieces, count, share):
    hidden = pieces.shape[1] // 2
    pieces = pieces.reshape(-1, share, 2 * hidden)
    results = [
        jax.ShapeDtypeStruct((count, share, 2 * hidden), jnp.bfloat16),
        jax.ShapeDtypeStruct((share, hidden), jnp.float32),
    ]
    copies, derivative = kernel_call(gelu_kernel, results, (pieces,), pieces.size)
    return copies.reshape(-1, 2 * hidden), derivative


def staged_then_direct(joined, share):
    pieces = exchange(joined, ("x",)).reshape(4, -1, joined.shape[1])
    results = [jax.ShapeDtypeStruct(pieces.shape[1:], jnp.bfloat16)]
    (partial,) = kernel_call(partial_sum_kernel, results, (pieces,), pieces.size)
    copies, derivative = apply_gelu(exchange(partial, ("zh",)), 16, share)
    return exchange(copies, ROWS), derivative


def direct_then_staged(joined, share):
    copies, derivative = apply_gelu(exchange(joined, ROWS), 4, share)
    block = exchange(copies, ("zh",))
    copies = jnp.broadcast_to(block[None], (4,) + block.shape).reshape(-1, block.shape[1])
    return exchange(copies, ("x",)), derivative


def swap_cores(block):
    return lax.ppermute(block, "c", SWAP)


def on_device(tokens, weight_in, tangent_in, weight_out, tangent_out, curvature):
    core = lax.axis_index("c")
    hidden = weight_in.shape[1]
    features = tokens.shape[1]
    share = tokens.shape[0] // 2

    halves = tokens.reshape(2, 1, share, features)
    copies = jnp.broadcast_to(halves, (2, lax.axis_size(TENSOR), share, features))
    arrived = exchange(copies.reshape(-1, features), ("c",) + TENSOR).reshape(2, -1, features)
    tokens_own = lax.dynamic_index_in_dim(arrived, core, 0, keepdims=False)
    tokens_far = lax.dynamic_index_in_dim(arrived, 1 - core, 0, keepdims=False)
    in_far, slope_far = swap_cores(weight_in), swap_cores(tangent_in)
    out_far, turn_far = swap_cores(weight_out), swap_cores(tangent_out)
    curvature_far = swap_cores(curvature)

    rows = arrived.shape[1]
    flops = 4 * rows * features * hidden
    preact, tangent = dot(tokens_own, weight_in), dot(tokens_own, tangent_in)
    (joined,) = kernel_call(
        far_products_kernel,
        [jax.ShapeDtypeStruct((rows, 2 * hidden), jnp.bfloat16)],
        (tokens_far, in_far, slope_far, preact, tangent),
        flops,
    )
    joined, out_far, turn_far, curvature_far = lax.optimization_barrier(
        (joined, out_far, turn_far, curvature_far)
    )
    both, derivative = lax.cond(
        core == 1,
        lambda j: staged_then_direct(j, share),
        lambda j: direct_then_staged(j, share),
        joined,
    )
    active = both[:, hidden:]

    (output_tangent,) = kernel_call(
        both_products_kernel,
        [jax.ShapeDtypeStruct((rows, 2 * features), jnp.bfloat16)],
        (both, weight_out, tangent_out, out_far, turn_far),
        2 * flops,
    )
    pieces = exchange(output_tangent, TENSOR).reshape(-1, share, 2 * features)
    (copies,) = kernel_call(
        cotangent_kernel,
        [jax.ShapeDtypeStruct(pieces.shape, jnp.bfloat16)],
        (pieces, curvature, curvature_far),
        pieces.size,
    )
    cotangent = exchange(copies.reshape(rows, 2 * features), TENSOR)
    cotangent_own, cotangent_far = cotangent[:, :features], cotangent[:, features:]

    (backward,) = kernel_call(
        backward_kernel,
        [jax.ShapeDtypeStruct((rows, hidden), jnp.bfloat16)],
        (cotangent, weight_out, out_far),
        flops,
    )
    pieces = exchange(backward, ROWS).reshape(-1, share, hidden)
    far_out = swap_cores(dot(active, cotangent_far, 0, 0).astype(jnp.bfloat16))
    product_out = dot(active, cotangent_own, 0, 0) + far_out.astype(jnp.float32)

    (copies,) = kernel_call(
        hidden_grad_kernel,
        [jax.ShapeDtypeStruct(pieces.shape, jnp.bfloat16)],
        (pieces, derivative),
        pieces.size,
    )
    hidden_grad = exchange(copies.reshape(rows, hidden), ROWS)
    product_out = product_out.astype(jnp.bfloat16)
    sent, far_out = lax.optimization_barrier((tokens_far, far_out))
    tokens_cross = swap_cores(sent)
    hidden_grad, product_out, tokens_cross = lax.optimization_barrier(
        (hidden_grad, product_out, tokens_cross)
    )
    far_grad = swap_cores(hidden_grad)
    own_in = lax.optimization_barrier(dot(tokens_own, hidden_grad, 0, 0))
    product_in = (own_in + dot(tokens_cross, far_grad, 0, 0)).astype(jnp.bfloat16)
    return (product_in, product_out)


def solution(mesh):
    fine = Mesh(mesh.devices.reshape(4, 4, 2, 8, 2), ("zh", "x", "c", "y", "zl"))
    by_dp = ("zh", "x", "c")
    return jax.shard_map(
        on_device,
        mesh=fine,
        in_specs=(
            P(TENSOR, by_dp),
            P(by_dp, TENSOR),
            P(by_dp, TENSOR),
            P(TENSOR, by_dp),
            P(TENSOR, by_dp),
            P(TENSOR, by_dp),
        ),
        out_specs=(P(by_dp, TENSOR), P(TENSOR, by_dp)),
        check_vma=False,
    )
```
